32 devices in a mesh: space: 16 (over z, x, core), chan: 2 (over y).
Axes of the slice: x: 2, y: 2, z: 4, core: 2. Of those that a mesh axis runs over, the one named last changes fastest.
Arguments:
- features: bfloat16 [16384, 256], P('space', 'chan'), may hold values from -6 to 6
- weights: bfloat16 [27, 256, 256], P(None, 'chan'), may hold values from -0.125 to 0.125
- send_rows: int32 [16, 8, 768], P('space'), may hold values from 0 to 1024, as said below
- gather_map: int32 [27, 16384], P(None, 'space'), may hold values from 0 to 7168, as said below
Outputs:
- output: bfloat16 [16384, 256], P('space', 'chan')
The draws below stay inside these ranges and needn't reach their ends.
Inputs may be any that keep to these rules, and one draw needn't show every extreme that they name: `send_rows`: an entry of 1024 marks an empty slot; the others are local row numbers of the sending block. Every direction of every block has some empty slots. `gather_map`: an entry of 7168 names the zero row; offset 13 (the centre) maps each voxel to its own local row.
All inputs are finite; a program needn't handle non-finite values.
Results may differ from the reference program's by a relative error of at most 0.001.
Values may be sent and summed in bfloat16 or wider, within the bound.
A program may use at most 64 MiB of HBM per device.

```python
import jax
import jax.numpy as jnp
from jax import lax

C = 256
OFFSETS = 27
GRID_COLS = 8
V_DEV = 1024
HALO = 768
BLOCKS = 16
VOX = 16384


def draw_send_rows(key, part):
    first, second = jax.random.split(jax.random.fold_in(key, 11))
    counts = jax.random.randint(first, (BLOCKS, 8, 1), HALO // 4, HALO)
    local_rows = jax.random.randint(second, (BLOCKS, 8, HALO), 0, V_DEV)
    slot = jnp.arange(HALO, dtype=jnp.int32)[None, None, :]
    return jnp.where(slot < counts, local_rows, V_DEV).astype(jnp.int32)


def draw_gather_map(key, part):
    first, second, third = jax.random.split(jax.random.fold_in(key, 23), 3)
    kind_of = jax.random.randint(first, (OFFSETS, VOX), 0, 4)
    local_rows = jax.random.randint(second, (OFFSETS, VOX), 0, V_DEV)
    remote_rows = V_DEV + jax.random.randint(third, (OFFSETS, VOX), 0, 8 * HALO)
    empty_row = V_DEV + 8 * HALO
    picked = jnp.where(kind_of < 2, local_rows, jnp.where(kind_of == 2, remote_rows, empty_row))
    own_rows = (jnp.arange(VOX, dtype=jnp.int32) % V_DEV)[None, :]
    centre = (jnp.arange(OFFSETS, dtype=jnp.int32) == 13)[:, None]
    return jnp.where(centre, own_rows, picked).astype(jnp.int32)


def spiked(array, key, source, target, shards_of, factor):
    owner, partner = [(jnp.arange(array.shape[axis_at]) // (array.shape[axis_at] // shards_of)).reshape([-1 if axis == axis_at else 1 for axis in range(array.ndim)]) for axis_at in (source, target)]
    chosen = jax.random.permutation(key, shards_of)[partner]
    strong = (owner == chosen) | (owner == (partner + shards_of // 2) % shards_of)
    return jnp.where(strong, factor * array, array)


def shard_levels(stream_key, extent, cuts, least, largest):
    level = 1.0
    for dim, shards_of in cuts:
        draws = jax.random.uniform(jax.random.fold_in(jax.random.fold_in(stream_key, 6), dim), (shards_of,), jnp.float32, least / len(cuts), largest / len(cuts))
        level = level * jnp.repeat(jnp.exp(draws), extent[dim] // shards_of).reshape((-1,) + (1,) * (len(extent) - 1 - dim))
    return level


def centred(key, shape, spread, limit, cuts=(), held_as=jnp.bfloat16):
    drawn = jax.random.normal(key, shape, jnp.float32) * spread
    if len(cuts) > 0:
        drawn = shard_levels(key, shape, cuts, -0.22, 0.18) * drawn
    return jnp.clip(drawn, min=-limit, max=limit).astype(held_as)


def gaussian_with(own_key, dims, scale, reach, cuts, heavy, kind=jnp.bfloat16):
    values = scale * jax.random.normal(own_key, dims, jnp.float32)
    if cuts:
        values = values * shard_levels(own_key, dims, cuts, -0.22, 0.18)
    return jnp.clip(spiked(values, jax.random.fold_in(own_key, 3), *heavy), -reach, reach).astype(kind)


def setup_inputs(seed: int = 0) -> dict:
    splits = jax.random.split(jax.random.key(seed), 5)
    features = centred(splits[0], (VOX, C), 1.0, 6.0, ((0, 16), (1, 2)))
    weights = gaussian_with(splits[1], (OFFSETS, C, C), (14 * C) ** -0.5, 0.125, ((1, 2),), (1, 2, 2, 2.0))
    send_rows = draw_send_rows(jax.random.fold_in(splits[4], 71), 0)
    gather_map = draw_gather_map(jax.random.fold_in(splits[4], 71), 0)
    return {"features": features, "weights": weights, "send_rows": send_rows, "gather_map": gather_map}


directions = [(-1, -1), (-1, 0), (-1, 1), (0, -1), (0, 1), (1, -1), (1, 0), (1, 1)]


def reference(features, weights, send_rows, gather_map):
    grid_rows = BLOCKS // GRID_COLS
    blocked = features.reshape(BLOCKS, V_DEV, C)
    padded = jnp.concatenate([blocked, jnp.zeros((BLOCKS, 1, C), jnp.bfloat16)], axis=1)
    kernel = weights.astype(jnp.float32)

    def one_block(block):
        block_row = block // GRID_COLS
        block_col = block % GRID_COLS
        pieces = [padded[block, :V_DEV]]
        for number, (step_x, step_y) in enumerate(directions):
            src_row = block_row - step_x
            src_col = block_col - step_y
            inside = (src_row >= 0) & (src_row < grid_rows) & (src_col >= 0) & (src_col < GRID_COLS)
            source = jnp.clip(src_row * GRID_COLS + src_col, 0, BLOCKS - 1).astype(jnp.int32)
            wanted = send_rows[source, number]
            got = padded[source][wanted]
            pieces.append(jnp.where(inside, got, jnp.zeros_like(got)))
        pieces.append(jnp.zeros((1, C), jnp.bfloat16))
        table = jnp.concatenate(pieces, axis=0)
        index = lax.dynamic_slice_in_dim(gather_map, (block * V_DEV).astype(jnp.int32), V_DEV, 1)
        picked = table[index].astype(jnp.float32)
        total = jnp.einsum("kvc,kco->vo", picked, kernel)
        return total.astype(jnp.bfloat16)

    result = lax.map(one_block, jnp.arange(BLOCKS, dtype=jnp.int32))
    return result.reshape(VOX, C)
```

```python
import functools

import jax
import jax.numpy as jnp
from jax import lax
from jax.experimental import pallas as pl
from jax.experimental.pallas import tpu as pltpu
from jax.sharding import PartitionSpec as P

GRID_COLS = 8
MESH = pl.DeviceIdType.MESH
DIRECTIONS = [(-1, -1), (-1, 0), (-1, 1), (0, -1), (0, 1), (1, -1), (1, 0), (1, 1)]
VERTICAL = {1: (0, 2), 6: (5, 7)}
HORIZONTAL = (3, 4)
LANES = 128
PIECES = 4
CHUNK = 256


def kernel(
    grid_rows, paired, feat, weights, send_rows, gmap, out,
    blocks, rows, lut, table, idx, idx_s, buf_a, buf_b, acc, own, outgoing, incoming,
    blk_send, blk_recv, row_send, row_recv, idx_sem, part_send, part_recv,
):
    voxels = feat.shape[0]
    offsets = gmap.shape[0]
    slot_tiles = rows.shape[1]
    zero_row = 9 * voxels
    piece = voxels // PIECES
    me = lax.axis_index("space")
    chan = lax.axis_index("chan")
    my_row = me // GRID_COLS
    my_col = me % GRID_COLS

    def inside(dx, dy):
        row, col = my_row + dx, my_col + dy
        return (row >= 0) & (row < grid_rows) & (col >= 0) & (col < GRID_COLS)

    def device(dx, dy):
        return (me + dx * GRID_COLS + dy, chan)

    def block_copy(src, slot, part, dx, dy):
        return pltpu.make_async_remote_copy(
            src_ref=src.at[pl.ds(part * piece, piece)],
            dst_ref=blocks.at[slot, pl.ds(part * piece, piece)],
            send_sem=blk_send.at[slot, part],
            recv_sem=blk_recv.at[slot, part],
            device_id=device(dx, dy),
            device_id_type=MESH,
        )

    def rows_copy(slot, dx, dy):
        return pltpu.make_async_remote_copy(
            src_ref=send_rows.at[slot],
            dst_ref=rows.at[slot],
            send_sem=row_send.at[slot],
            recv_sem=row_recv.at[slot],
            device_id=device(dx, dy),
            device_id_type=MESH,
        )

    rows[...] = jnp.full(rows.shape, voxels, jnp.int32)

    barrier = pltpu.get_barrier_semaphore()
    expected = jnp.int32(1 if paired else 0)
    for dx, dy in DIRECTIONS:
        expected = expected + inside(dx, dy).astype(jnp.int32)

        @pl.when(inside(dx, dy))
        def _():
            pl.semaphore_signal(barrier, inc=1, device_id=device(dx, dy), device_id_type=MESH)

    if paired:
        pl.semaphore_signal(barrier, inc=1, device_id=(me, 1 - chan), device_id_type=MESH)
    pl.semaphore_wait(barrier, expected)

    for part in range(PIECES):
        for slot in VERTICAL:
            dx, dy = DIRECTIONS[slot]

            @pl.when(inside(dx, dy))
            def _():
                if part == 0:
                    rows_copy(slot, dx, dy).start()
                block_copy(feat, slot, part, dx, dy).start()

    for slot, (dx, dy) in enumerate(DIRECTIONS):
        if slot in VERTICAL:
            continue

        @pl.when(inside(dx, dy))
        def _():
            rows_copy(slot, dx, dy).start()
            if slot in HORIZONTAL:
                for part in range(PIECES):
                    block_copy(feat, slot, part, dx, dy).start()

    def widen(src, number, part):
        table[pl.ds(number * voxels + part * piece, piece), :] = src[pl.ds(part * piece, piece), :].astype(jnp.float32)

    table[pl.ds(zero_row, 8), :] = jnp.zeros((8, LANES), jnp.float32)
    for part in range(PIECES):
        widen(feat, 0, part)

    for slot, (dx, dy) in enumerate(DIRECTIONS):
        @pl.when(inside(-dx, -dy))
        def _():
            rows_copy(slot, -dx, -dy).wait_recv()

        entry = rows[slot]
        lut[slot] = jnp.where(entry < voxels, entry + (1 + slot) * voxels, zero_row)

    own_tiles = voxels // LANES

    def compose(col, _):
        lanes = pl.ds(pl.multiple_of(col * LANES, LANES), LANES)
        starts = list(range(0, offsets - 7, 8))
        if offsets % 8:
            starts.append(offsets - 8)
        entries = [gmap[pl.ds(start, 8), lanes] for start in starts]
        within = [entry & (LANES - 1) for entry in entries]
        tiles = [entry >> 7 for entry in entries]
        result = [jnp.where(entry < voxels, entry, zero_row) for entry in entries]
        for slot in range(8):
            for tile in range(slot_tiles):
                line = jnp.broadcast_to(lut[slot, pl.ds(tile, 1), :], (8, LANES))
                number = own_tiles + slot * slot_tiles + tile
                for i in range(len(starts)):
                    found = jnp.take_along_axis(line, within[i], axis=1, mode="promise_in_bounds")
                    result[i] = jnp.where(tiles[i] == number, found, result[i])
        for start, value in zip(starts, result):
            idx[pl.ds(start, 8), lanes] = value
        return 0

    lax.fori_loop(0, own_tiles, compose, 0)
    to_scalar = pltpu.make_async_copy(idx, idx_s, idx_sem)
    to_scalar.start()

    for part in range(PIECES):
        for slot, (left, right) in VERTICAL.items():
            dx, dy = DIRECTIONS[slot]

            @pl.when(inside(-dx, -dy))
            def _():
                block_copy(feat, slot, part, -dx, -dy).wait_recv()
                for target, step in ((left, -1), (right, 1)):
                    @pl.when(inside(0, step))
                    def _():
                        block_copy(blocks.at[slot], target, part, 0, step).start()

                widen(blocks.at[slot], 1 + slot, part)

    for slot in HORIZONTAL + (0, 2, 5, 7):
        dx, dy = DIRECTIONS[slot]

        @pl.when(inside(-dx, -dy))
        def _():
            for part in range(PIECES):
                block_copy(feat, slot, part, -dx, -dy).wait_recv()
                widen(blocks.at[slot], 1 + slot, part)

    to_scalar.wait()

    def gather(buf, first, count, base):
        for half in range(count):
            for v in range(CHUNK):
                row = idx_s[first + half, base + v]
                buf[pl.ds(v, 1), pl.ds(half * LANES, LANES)] = table[pl.ds(row, 1), :]

    def product(buf, pair, base):
        kernel_pair = weights[pl.ds(2 * pair, 2)].reshape(2 * LANES, weights.shape[2])
        acc[...] += jnp.dot(buf[...].astype(jnp.bfloat16), kernel_pair, preferred_element_type=jnp.float32)

    pairs = offsets // 2
    other = pl.ds(pl.multiple_of((1 - chan) * LANES, LANES), LANES)
    mine = pl.ds(pl.multiple_of(chan * LANES, LANES), LANES)

    def partial_copy(chunk):
        span = pl.ds(pl.multiple_of(chunk * CHUNK, CHUNK), CHUNK)
        return pltpu.make_async_remote_copy(
            src_ref=outgoing.at[span],
            dst_ref=incoming.at[span],
            send_sem=part_send.at[chunk],
            recv_sem=part_recv.at[chunk],
            device_id=(me, 1 - chan),
            device_id_type=MESH,
        )

    def step(chunk, _):
        base = chunk * CHUNK
        span = pl.ds(pl.multiple_of(base, CHUNK), CHUNK)
        acc[...] = jnp.zeros_like(acc)
        gather(buf_a, 0, 2, base)

        def two(i, _):
            product(buf_a, 2 * i, base)
            gather(buf_b, 4 * i + 2, 2, base)
            product(buf_b, 2 * i + 1, base)
            gather(buf_a, 4 * i + 4, 2, base)
            return 0

        lax.fori_loop(0, (pairs - 1) // 2, two, 0)
        product(buf_a, pairs - 1, base)
        gather(buf_b, offsets - 1, 1, base)
        total = acc[...] + jnp.dot(
            buf_b[:, pl.ds(0, LANES)].astype(jnp.bfloat16), weights[offsets - 1], preferred_element_type=jnp.float32
        )
        if not paired:
            out[span, :] = total
            return 0
        acc[...] = total
        own[span, :] = acc[:, mine]
        outgoing[span, :] = acc[:, other]
        partial_copy(chunk).start()
        return 0

    chunks = voxels // CHUNK
    lax.fori_loop(0, chunks, step, 0)

    def finish(chunk, _):
        span = pl.ds(pl.multiple_of(chunk * CHUNK, CHUNK), CHUNK)
        partial_copy(chunk).wait()
        out[span, :] = (own[span, :] + incoming[span, :]).astype(out.dtype)
        return 0

    if paired:
        lax.fori_loop(0, chunks, finish, 0)

    for slot, (dx, dy) in enumerate(DIRECTIONS):
        @pl.when(inside(dx, dy))
        def _():
            rows_copy(slot, dx, dy).wait_send()
            if slot in VERTICAL or slot in HORIZONTAL:
                for part in range(PIECES):
                    block_copy(feat, slot, part, dx, dy).wait_send()

    for slot, targets in VERTICAL.items():
        dx, dy = DIRECTIONS[slot]
        for target, step_y in zip(targets, (-1, 1)):
            @pl.when(inside(-dx, -dy) & inside(0, step_y))
            def _():
                for part in range(PIECES):
                    block_copy(feat, target, part, 0, step_y).wait_send()


def local(grid_rows, features, weights, send_rows, gather_map):
    voxels, own_width = features.shape
    offsets = gather_map.shape[0]
    out_width = weights.shape[2]
    slots = send_rows.shape[2]
    lines = send_rows.reshape(8, slots // LANES, LANES)
    paired = lax.axis_size("chan") == 2 and own_width == LANES
    if not paired:
        features = jnp.pad(features, ((0, 0), (0, LANES - own_width)))
        weights = jnp.pad(weights, ((0, 0), (0, LANES - own_width), (0, 0)))
    width = LANES
    chunks = voxels // CHUNK
    dma = pltpu.SemaphoreType.DMA
    result = jax.ShapeDtypeStruct((voxels, width) if paired else (voxels, out_width), jnp.bfloat16 if paired else jnp.float32)
    made = pl.pallas_call(
        functools.partial(kernel, grid_rows, paired),
        out_shape=result,
        in_specs=[pl.BlockSpec(memory_space=pltpu.VMEM)] * 4,
        out_specs=pl.BlockSpec(memory_space=pltpu.VMEM),
        scratch_shapes=[
            pltpu.VMEM((8, voxels, width), jnp.bfloat16),
            pltpu.VMEM(lines.shape, jnp.int32),
            pltpu.VMEM(lines.shape, jnp.int32),
            pltpu.VMEM((9 * voxels + 8, width), jnp.float32),
            pltpu.VMEM((offsets, voxels), jnp.int32),
            pltpu.SMEM((offsets, voxels), jnp.int32),
            pltpu.VMEM((CHUNK, 2 * width), jnp.float32),
            pltpu.VMEM((CHUNK, 2 * width), jnp.float32),
            pltpu.VMEM((CHUNK, out_width), jnp.float32),
            pltpu.VMEM((voxels, width), jnp.float32),
            pltpu.VMEM((voxels, width), jnp.float32),
            pltpu.VMEM((voxels, width), jnp.float32),
            dma((8, PIECES)), dma((8, PIECES)), dma((8,)), dma((8,)), dma, dma((chunks,)), dma((chunks,)),
        ],
        compiler_params=pltpu.CompilerParams(
            collective_id=0, has_side_effects=True, vmem_limit_bytes=40 * 1024 * 1024
        ),
        cost_estimate=pl.CostEstimate(
            flops=2 * voxels * offsets * width * out_width, bytes_accessed=6 * 1024 * 1024, transcendentals=0
        ),
    )(features, weights, lines, gather_map)
    if paired:
        return made
    return lax.psum_scatter(made, "chan", scatter_dimension=1, tiled=True).astype(jnp.bfloat16)


def solution(mesh):
    grid_rows = mesh.shape["space"] // GRID_COLS
    in_specs = (P("space", "chan"), P(None, "chan", None), P("space", None, None), P(None, "space"))
    out_specs = P("space", "chan")
    return jax.shard_map(
        functools.partial(local, grid_rows), mesh=mesh, in_specs=in_specs, out_specs=out_specs, check_vma=False
    )
```

```python
import functools

import jax
import jax.numpy as jnp
from jax import lax
from jax.experimental import pallas as pl
from jax.experimental.pallas import tpu as pltpu
from jax.sharding import PartitionSpec as P

GRID_COLS = 8
MESH = pl.DeviceIdType.MESH
DIRECTIONS = [(-1, -1), (-1, 0), (-1, 1), (0, -1), (0, 1), (1, -1), (1, 0), (1, 1)]
VERTICAL = {1: (0, 2), 6: (5, 7)}
HORIZONTAL = (3, 4)
LANES = 128
PIECES = 4
CHUNK = 256
GROUP = 32


def kernel(
    grid_rows, paired, feat_hbm, weights_hbm, send_rows, gmap_hbm, out,
    feat, weights, gmap, blocks, rows, lut, table, idx, idx_s, buf_a, buf_b, acc, own, outgoing, incoming,
    blk_send, blk_recv, row_send, row_recv, in_sem, idx_sem, part_send, part_recv,
):
    voxels = feat.shape[0]
    offsets = gmap.shape[0]
    slot_tiles = rows.shape[2] // LANES
    zero_row = 9 * voxels
    piece = voxels // PIECES
    me = lax.axis_index("space")
    chan = lax.axis_index("chan")
    my_row = me // GRID_COLS
    my_col = me % GRID_COLS

    def inside(dx, dy):
        row, col = my_row + dx, my_col + dy
        return (row >= 0) & (row < grid_rows) & (col >= 0) & (col < GRID_COLS)

    def device(dx, dy):
        return (me + dx * GRID_COLS + dy, chan)

    def block_copy(src, slot, part, dx, dy):
        return pltpu.make_async_remote_copy(
            src_ref=src.at[pl.ds(part * piece, piece)],
            dst_ref=blocks.at[slot, pl.ds(part * piece, piece)],
            send_sem=blk_send.at[slot, part],
            recv_sem=blk_recv.at[slot, part],
            device_id=device(dx, dy),
            device_id_type=MESH,
        )

    def rows_copy(slot, dx, dy):
        return pltpu.make_async_remote_copy(
            src_ref=send_rows.at[0, pl.ds(slot, 1)],
            dst_ref=rows.at[slot],
            send_sem=row_send.at[slot],
            recv_sem=row_recv.at[slot],
            device_id=device(dx, dy),
            device_id_type=MESH,
        )

    staged = [
        pltpu.make_async_copy(source, target, in_sem.at[number])
        for number, (source, target) in enumerate(((feat_hbm, feat), (gmap_hbm, gmap), (weights_hbm, weights)))
    ]
    for copy in staged:
        copy.start()

    rows[...] = jnp.full(rows.shape, voxels, jnp.int32)

    barrier = pltpu.get_barrier_semaphore()
    expected = jnp.int32(1 if paired else 0)
    for dx, dy in DIRECTIONS:
        expected = expected + inside(dx, dy).astype(jnp.int32)

        @pl.when(inside(dx, dy))
        def _():
            pl.semaphore_signal(barrier, inc=1, device_id=device(dx, dy), device_id_type=MESH)

    if paired:
        pl.semaphore_signal(barrier, inc=1, device_id=(me, 1 - chan), device_id_type=MESH)
    pl.semaphore_wait(barrier, expected)

    for part in range(PIECES):
        for slot in VERTICAL:
            dx, dy = DIRECTIONS[slot]

            @pl.when(inside(dx, dy))
            def _():
                if part == 0:
                    rows_copy(slot, dx, dy).start()
                block_copy(feat_hbm, slot, part, dx, dy).start()

    for slot, (dx, dy) in enumerate(DIRECTIONS):
        if slot in VERTICAL:
            continue

        @pl.when(inside(dx, dy))
        def _():
            rows_copy(slot, dx, dy).start()
            if slot in HORIZONTAL:
                for part in range(PIECES):
                    block_copy(feat_hbm, slot, part, dx, dy).start()

    def widen(src, number, part):
        table[pl.ds(number * voxels + part * piece, piece), :] = src[pl.ds(part * piece, piece), :].astype(jnp.float32)

    table[pl.ds(zero_row, 8), :] = jnp.zeros((8, LANES), jnp.float32)
    staged[0].wait()
    for part in range(PIECES):
        widen(feat, 0, part)
    staged[1].wait()

    for slot, (dx, dy) in enumerate(DIRECTIONS):
        @pl.when(inside(-dx, -dy))
        def _():
            rows_copy(slot, -dx, -dy).wait_recv()

        entry = rows[slot]
        lut[slot] = jnp.where(entry < voxels, entry + (1 + slot) * voxels, zero_row)

    own_tiles = voxels // LANES

    def compose(col, _):
        lanes = pl.ds(pl.multiple_of(col * LANES, LANES), LANES)
        starts = list(range(0, offsets - 7, 8))
        if offsets % 8:
            starts.append(offsets - 8)
        entries = [gmap[pl.ds(start, 8), lanes] for start in starts]
        within = [entry & (LANES - 1) for entry in entries]
        tiles = [entry >> 7 for entry in entries]
        result = [jnp.where(entry < voxels, entry, zero_row) for entry in entries]
        for slot in range(8):
            for tile in range(slot_tiles):
                line = jnp.broadcast_to(lut[slot, :, pl.ds(tile * LANES, LANES)], (8, LANES))
                number = own_tiles + slot * slot_tiles + tile
                for i in range(len(starts)):
                    found = jnp.take_along_axis(line, within[i], axis=1, mode="promise_in_bounds")
                    result[i] = jnp.where(tiles[i] == number, found, result[i])
        for start, value in zip(starts, result):
            idx[pl.ds(start, 8), lanes] = value
        return 0

    lax.fori_loop(0, own_tiles, compose, 0)
    to_scalar = pltpu.make_async_copy(idx, idx_s, idx_sem)
    to_scalar.start()

    for part in range(PIECES):
        for slot, (left, right) in VERTICAL.items():
            dx, dy = DIRECTIONS[slot]

            @pl.when(inside(-dx, -dy))
            def _():
                block_copy(feat, slot, part, -dx, -dy).wait_recv()
                for target, step in ((left, -1), (right, 1)):
                    @pl.when(inside(0, step))
                    def _():
                        block_copy(blocks.at[slot], target, part, 0, step).start()

                widen(blocks.at[slot], 1 + slot, part)

    for slot in HORIZONTAL + (0, 2, 5, 7):
        dx, dy = DIRECTIONS[slot]

        @pl.when(inside(-dx, -dy))
        def _():
            for part in range(PIECES):
                block_copy(feat, slot, part, -dx, -dy).wait_recv()
                widen(blocks.at[slot], 1 + slot, part)

    to_scalar.wait()
    staged[2].wait()

    centre = offsets // 2
    pairs = centre

    def offset_of(number):
        return number + (number >= centre).astype(jnp.int32)

    def gather(buf, pair, base):
        for half in range(2):
            offset = offset_of(2 * pair + half)
            for first in range(0, CHUNK, GROUP):
                taken = [table[pl.ds(idx_s[offset, base + first + v], 1), :] for v in range(GROUP)]
                for v in range(GROUP):
                    buf[pl.ds(first + v, 1), pl.ds(half * LANES, LANES)] = taken[v]

    def product(buf, pair):
        kernel_pair = jnp.concatenate([weights[offset_of(2 * pair)], weights[offset_of(2 * pair + 1)]], axis=0)
        acc[...] += jnp.dot(buf[...].astype(jnp.bfloat16), kernel_pair, preferred_element_type=jnp.float32)

    other = pl.ds(pl.multiple_of((1 - chan) * LANES, LANES), LANES)
    mine = pl.ds(pl.multiple_of(chan * LANES, LANES), LANES)

    def partial_copy(chunk):
        span = pl.ds(pl.multiple_of(chunk * CHUNK, CHUNK), CHUNK)
        return pltpu.make_async_remote_copy(
            src_ref=outgoing.at[span],
            dst_ref=incoming.at[span],
            send_sem=part_send.at[chunk],
            recv_sem=part_recv.at[chunk],
            device_id=(me, 1 - chan),
            device_id_type=MESH,
        )

    def step(chunk, _):
        base = chunk * CHUNK
        span = pl.ds(pl.multiple_of(base, CHUNK), CHUNK)
        acc[...] = jnp.dot(feat[span, :], weights[centre], preferred_element_type=jnp.float32)
        gather(buf_a, jnp.int32(0), base)

        def two(i, _):
            product(buf_a, 2 * i)
            gather(buf_b, 2 * i + 1, base)
            product(buf_b, 2 * i + 1)
            gather(buf_a, 2 * i + 2, base)
            return 0

        lax.fori_loop(0, (pairs - 1) // 2, two, 0)
        product(buf_a, jnp.int32(pairs - 1))
        if not paired:
            out[span, :] = acc[...]
            return 0
        own[span, :] = acc[:, mine]
        outgoing[span, :] = acc[:, other]
        partial_copy(chunk).start()
        return 0

    chunks = voxels // CHUNK
    lax.fori_loop(0, chunks, step, 0)

    def finish(chunk, _):
        span = pl.ds(pl.multiple_of(chunk * CHUNK, CHUNK), CHUNK)
        partial_copy(chunk).wait()
        out[span, :] = (own[span, :] + incoming[span, :]).astype(out.dtype)
        return 0

    if paired:
        lax.fori_loop(0, chunks, finish, 0)

    for slot, (dx, dy) in enumerate(DIRECTIONS):
        @pl.when(inside(dx, dy))
        def _():
            rows_copy(slot, dx, dy).wait_send()
            if slot in VERTICAL or slot in HORIZONTAL:
                for part in range(PIECES):
                    block_copy(feat, slot, part, dx, dy).wait_send()

    for slot, targets in VERTICAL.items():
        dx, dy = DIRECTIONS[slot]
        for target, step_y in zip(targets, (-1, 1)):
            @pl.when(inside(-dx, -dy) & inside(0, step_y))
            def _():
                for part in range(PIECES):
                    block_copy(feat, target, part, 0, step_y).wait_send()


def local(grid_rows, features, weights, send_rows, gather_map):
    voxels, own_width = features.shape
    offsets = gather_map.shape[0]
    out_width = weights.shape[2]
    slots = send_rows.shape[2]
    paired = lax.axis_size("chan") == 2 and own_width == LANES
    if not paired:
        features = jnp.pad(features, ((0, 0), (0, LANES - own_width)))
        weights = jnp.pad(weights, ((0, 0), (0, LANES - own_width), (0, 0)))
    width = LANES
    chunks = voxels // CHUNK
    dma = pltpu.SemaphoreType.DMA
    result = jax.ShapeDtypeStruct((voxels, width) if paired else (voxels, out_width), jnp.bfloat16 if paired else jnp.float32)
    made = pl.pallas_call(
        functools.partial(kernel, grid_rows, paired),
        out_shape=result,
        in_specs=[pl.BlockSpec(memory_space=pl.ANY)] * 4,
        out_specs=pl.BlockSpec(memory_space=pltpu.VMEM),
        scratch_shapes=[
            pltpu.VMEM(features.shape, features.dtype),
            pltpu.VMEM(weights.shape, weights.dtype),
            pltpu.VMEM(gather_map.shape, gather_map.dtype),
            pltpu.VMEM((8, voxels, width), jnp.bfloat16),
            pltpu.VMEM((8, 1, slots), jnp.int32),
            pltpu.VMEM((8, 1, slots), jnp.int32),
            pltpu.VMEM((9 * voxels + 8, width), jnp.float32),
            pltpu.VMEM((offsets, voxels), jnp.int32),
            pltpu.SMEM((offsets, voxels), jnp.int32),
            pltpu.VMEM((CHUNK, 2 * width), jnp.float32),
            pltpu.VMEM((CHUNK, 2 * width), jnp.float32),
            pltpu.VMEM((CHUNK, out_width), jnp.float32),
            pltpu.VMEM((voxels, width), jnp.float32),
            pltpu.VMEM((voxels, width), jnp.float32),
            pltpu.VMEM((voxels, width), jnp.float32),
            dma((8, PIECES)), dma((8, PIECES)), dma((8,)), dma((8,)), dma((3,)), dma, dma((chunks,)), dma((chunks,)),
        ],
        compiler_params=pltpu.CompilerParams(
            collective_id=0, has_side_effects=True, vmem_limit_bytes=40 * 1024 * 1024
        ),
        cost_estimate=pl.CostEstimate(
            flops=2 * voxels * offsets * width * out_width, bytes_accessed=6 * 1024 * 1024, transcendentals=0
        ),
    )(features, weights, send_rows, gather_map)
    if paired:
        return made
    return lax.psum_scatter(made, "chan", scatter_dimension=1, tiled=True).astype(jnp.bfloat16)


def solution(mesh):
    grid_rows = mesh.shape["space"] // GRID_COLS
    in_specs = (P("space", "chan"), P(None, "chan", None), P("space", None, None), P(None, "space"))
    out_specs = P("space", "chan")
    return jax.shard_map(
        functools.partial(local, grid_rows), mesh=mesh, in_specs=in_specs, out_specs=out_specs, check_vma=False
    )
```

```python
import functools

import jax
import jax.numpy as jnp
from jax import lax
from jax.experimental import pallas as pl
from jax.experimental.pallas import tpu as pltpu
from jax.sharding import PartitionSpec as P

GRID_COLS = 8
MESH = pl.DeviceIdType.MESH
DIRECTIONS = [(-1, -1), (-1, 0), (-1, 1), (0, -1), (0, 1), (1, -1), (1, 0), (1, 1)]
VERTICAL = {1: (0, 2), 6: (5, 7)}
HORIZONTAL = (3, 4)
LANES = 128
PIECES = 4
CHUNK = 256
GROUP = 32


def exchange(
    grid_rows, feat, send_rows, gmap, table, idx,
    blocks, rows, lut, blk_send, blk_recv, row_send, row_recv,
):
    voxels = feat.shape[0]
    offsets = gmap.shape[0]
    slot_tiles = rows.shape[2] // LANES
    zero_row = 9 * voxels
    piece = voxels // PIECES
    me = lax.axis_index("space")
    chan = lax.axis_index("chan")
    my_row = me // GRID_COLS
    my_col = me % GRID_COLS

    def inside(dx, dy):
        row, col = my_row + dx, my_col + dy
        return (row >= 0) & (row < grid_rows) & (col >= 0) & (col < GRID_COLS)

    def device(dx, dy):
        return (me + dx * GRID_COLS + dy, chan)

    def block_copy(src, slot, part, dx, dy):
        return pltpu.make_async_remote_copy(
            src_ref=src.at[pl.ds(part * piece, piece)],
            dst_ref=blocks.at[slot, pl.ds(part * piece, piece)],
            send_sem=blk_send.at[slot, part],
            recv_sem=blk_recv.at[slot, part],
            device_id=device(dx, dy),
            device_id_type=MESH,
        )

    def rows_copy(slot, dx, dy):
        return pltpu.make_async_remote_copy(
            src_ref=send_rows.at[0, pl.ds(slot, 1)],
            dst_ref=rows.at[slot],
            send_sem=row_send.at[slot],
            recv_sem=row_recv.at[slot],
            device_id=device(dx, dy),
            device_id_type=MESH,
        )

    rows[...] = jnp.full(rows.shape, voxels, jnp.int32)

    barrier = pltpu.get_barrier_semaphore()
    expected = jnp.int32(0)
    for dx, dy in DIRECTIONS:
        expected = expected + inside(dx, dy).astype(jnp.int32)

        @pl.when(inside(dx, dy))
        def _():
            pl.semaphore_signal(barrier, inc=1, device_id=device(dx, dy), device_id_type=MESH)

    pl.semaphore_wait(barrier, expected)

    for part in range(PIECES):
        for slot in VERTICAL:
            dx, dy = DIRECTIONS[slot]

            @pl.when(inside(dx, dy))
            def _():
                if part == 0:
                    rows_copy(slot, dx, dy).start()
                block_copy(feat, slot, part, dx, dy).start()

    for slot, (dx, dy) in enumerate(DIRECTIONS):
        if slot in VERTICAL:
            continue

        @pl.when(inside(dx, dy))
        def _():
            rows_copy(slot, dx, dy).start()
            if slot in HORIZONTAL:
                for part in range(PIECES):
                    block_copy(feat, slot, part, dx, dy).start()

    def widen(src, number, part):
        table[pl.ds(number * voxels + part * piece, piece), :] = src[pl.ds(part * piece, piece), :].astype(jnp.float32)

    table[pl.ds(zero_row, 8), :] = jnp.zeros((8, LANES), jnp.float32)
    for part in range(PIECES):
        widen(feat, 0, part)

    for slot, (dx, dy) in enumerate(DIRECTIONS):
        @pl.when(inside(-dx, -dy))
        def _():
            rows_copy(slot, -dx, -dy).wait_recv()

        entry = rows[slot]
        lut[slot] = jnp.where(entry < voxels, entry + (1 + slot) * voxels, zero_row)

    own_tiles = voxels // LANES

    def compose(col, _):
        lanes = pl.ds(pl.multiple_of(col * LANES, LANES), LANES)
        starts = list(range(0, offsets - 7, 8))
        if offsets % 8:
            starts.append(offsets - 8)
        entries = [gmap[pl.ds(start, 8), lanes] for start in starts]
        within = [entry & (LANES - 1) for entry in entries]
        tiles = [entry >> 7 for entry in entries]
        result = [jnp.where(entry < voxels, entry, zero_row) for entry in entries]
        for slot in range(8):
            for tile in range(slot_tiles):
                line = jnp.broadcast_to(lut[slot, :, pl.ds(tile * LANES, LANES)], (8, LANES))
                number = own_tiles + slot * slot_tiles + tile
                for i in range(len(starts)):
                    found = jnp.take_along_axis(line, within[i], axis=1, mode="promise_in_bounds")
                    result[i] = jnp.where(tiles[i] == number, found, result[i])
        for start, value in zip(starts, result):
            idx[pl.ds(start, 8), lanes] = value
        return 0

    lax.fori_loop(0, own_tiles, compose, 0)

    for part in range(PIECES):
        for slot, (left, right) in VERTICAL.items():
            dx, dy = DIRECTIONS[slot]

            @pl.when(inside(-dx, -dy))
            def _():
                block_copy(feat, slot, part, -dx, -dy).wait_recv()
                for target, step in ((left, -1), (right, 1)):
                    @pl.when(inside(0, step))
                    def _():
                        block_copy(blocks.at[slot], target, part, 0, step).start()

                widen(blocks.at[slot], 1 + slot, part)

    for slot in HORIZONTAL + (0, 2, 5, 7):
        dx, dy = DIRECTIONS[slot]

        @pl.when(inside(-dx, -dy))
        def _():
            for part in range(PIECES):
                block_copy(feat, slot, part, -dx, -dy).wait_recv()
                widen(blocks.at[slot], 1 + slot, part)

    for slot, (dx, dy) in enumerate(DIRECTIONS):
        @pl.when(inside(dx, dy))
        def _():
            rows_copy(slot, dx, dy).wait_send()
            if slot in VERTICAL or slot in HORIZONTAL:
                for part in range(PIECES):
                    block_copy(feat, slot, part, dx, dy).wait_send()

    for slot, targets in VERTICAL.items():
        dx, dy = DIRECTIONS[slot]
        for target, step_y in zip(targets, (-1, 1)):
            @pl.when(inside(-dx, -dy) & inside(0, step_y))
            def _():
                for part in range(PIECES):
                    block_copy(feat, target, part, 0, step_y).wait_send()


def convolve(paired, table, idx, feat, weights, out, idx_s, buf_a, buf_b, acc, own, outgoing, incoming, idx_sem, part_send, part_recv):
    voxels = feat.shape[0]
    offsets = weights.shape[0]
    me = lax.axis_index("space")
    chan = lax.axis_index("chan")
    to_scalar = pltpu.make_async_copy(idx, idx_s, idx_sem)
    to_scalar.start()
    if paired:
        barrier = pltpu.get_barrier_semaphore()
        pl.semaphore_signal(barrier, inc=1, device_id=(me, 1 - chan), device_id_type=MESH)
        pl.semaphore_wait(barrier, 1)
    to_scalar.wait()

    centre = offsets // 2
    pairs = centre

    def offset_of(number):
        return number + (number >= centre).astype(jnp.int32)

    def gather(buf, pair, base):
        for half in range(2):
            offset = offset_of(2 * pair + half)
            for first in range(0, CHUNK, GROUP):
                taken = [table[idx_s[offset, base + first + v]] for v in range(GROUP)]
                for v in range(GROUP):
                    buf[pl.ds(first + v, 1), pl.ds(half * LANES, LANES)] = taken[v]

    def product(buf, pair):
        kernel_pair = jnp.concatenate([weights[offset_of(2 * pair)], weights[offset_of(2 * pair + 1)]], axis=0)
        acc[...] += jnp.dot(buf[...].astype(jnp.bfloat16), kernel_pair, preferred_element_type=jnp.float32)

    other = pl.ds(pl.multiple_of((1 - chan) * LANES, LANES), LANES)
    mine = pl.ds(pl.multiple_of(chan * LANES, LANES), LANES)

    def partial_copy(chunk):
        span = pl.ds(pl.multiple_of(chunk * CHUNK, CHUNK), CHUNK)
        return pltpu.make_async_remote_copy(
            src_ref=outgoing.at[span],
            dst_ref=incoming.at[span],
            send_sem=part_send.at[chunk],
            recv_sem=part_recv.at[chunk],
            device_id=(me, 1 - chan),
            device_id_type=MESH,
        )

    def step(chunk, _):
        base = chunk * CHUNK
        span = pl.ds(pl.multiple_of(base, CHUNK), CHUNK)
        acc[...] = jnp.dot(feat[span, :], weights[centre], preferred_element_type=jnp.float32)
        gather(buf_a, jnp.int32(0), base)

        def two(i, _):
            product(buf_a, 2 * i)
            gather(buf_b, 2 * i + 1, base)
            product(buf_b, 2 * i + 1)
            gather(buf_a, 2 * i + 2, base)
            return 0

        lax.fori_loop(0, (pairs - 1) // 2, two, 0)
        product(buf_a, jnp.int32(pairs - 1))
        if not paired:
            out[span, :] = acc[...]
            return 0
        own[span, :] = acc[:, mine]
        outgoing[span, :] = acc[:, other]
        partial_copy(chunk).start()
        return 0

    chunks = voxels // CHUNK
    lax.fori_loop(0, chunks, step, 0)

    def finish(chunk, _):
        span = pl.ds(pl.multiple_of(chunk * CHUNK, CHUNK), CHUNK)
        partial_copy(chunk).wait()
        out[span, :] = (own[span, :] + incoming[span, :]).astype(out.dtype)
        return 0

    if paired:
        lax.fori_loop(0, chunks, finish, 0)


def local(grid_rows, features, weights, send_rows, gather_map):
    voxels, own_width = features.shape
    offsets = gather_map.shape[0]
    out_width = weights.shape[2]
    slots = send_rows.shape[2]
    paired = lax.axis_size("chan") == 2 and own_width == LANES
    if not paired:
        features = jnp.pad(features, ((0, 0), (0, LANES - own_width)))
        weights = jnp.pad(weights, ((0, 0), (0, LANES - own_width), (0, 0)))
    width = LANES
    chunks = voxels // CHUNK
    dma = pltpu.SemaphoreType.DMA
    result = jax.ShapeDtypeStruct((voxels, width) if paired else (voxels, out_width), jnp.bfloat16 if paired else jnp.float32)
    vmem = pl.BlockSpec(memory_space=pltpu.VMEM)
    table, idx = pl.pallas_call(
        functools.partial(exchange, grid_rows),
        out_shape=(
            jax.ShapeDtypeStruct((9 * voxels + 8, width), jnp.float32),
            jax.ShapeDtypeStruct((offsets, voxels), jnp.int32),
        ),
        in_specs=[vmem] * 3,
        out_specs=(vmem, vmem),
        scratch_shapes=[
            pltpu.VMEM((8, voxels, width), jnp.bfloat16),
            pltpu.VMEM((8, 1, slots), jnp.int32),
            pltpu.VMEM((8, 1, slots), jnp.int32),
            dma((8, PIECES)), dma((8, PIECES)), dma((8,)), dma((8,)),
        ],
        compiler_params=pltpu.CompilerParams(
            collective_id=0, has_side_effects=True, vmem_limit_bytes=20 * 1024 * 1024
        ),
        cost_estimate=pl.CostEstimate(flops=0, bytes_accessed=64 * 1024 * 1024, transcendentals=0),
    )(features, send_rows, gather_map)
    made = pl.pallas_call(
        functools.partial(convolve, paired),
        out_shape=result,
        in_specs=[vmem] * 4,
        out_specs=vmem,
        scratch_shapes=[
            pltpu.SMEM((offsets, voxels), jnp.int32),
            pltpu.VMEM((CHUNK, 2 * width), jnp.float32),
            pltpu.VMEM((CHUNK, 2 * width), jnp.float32),
            pltpu.VMEM((CHUNK, out_width), jnp.float32),
            pltpu.VMEM((voxels, width), jnp.float32),
            pltpu.VMEM((voxels, width), jnp.float32),
            pltpu.VMEM((voxels, width), jnp.float32),
            dma, dma((chunks,)), dma((chunks,)),
        ],
        compiler_params=pltpu.CompilerParams(
            collective_id=1 if paired else None, has_side_effects=paired, vmem_limit_bytes=24 * 1024 * 1024
        ),
        cost_estimate=pl.CostEstimate(
            flops=2 * voxels * offsets * width * out_width, bytes_accessed=8 * 1024 * 1024, transcendentals=0
        ),
    )(table.reshape(9 * voxels + 8, 1, width), idx, features, weights)
    if paired:
        return made
    return lax.psum_scatter(made, "chan", scatter_dimension=1, tiled=True).astype(jnp.bfloat16)


def solution(mesh):
    grid_rows = mesh.shape["space"] // GRID_COLS
    in_specs = (P("space", "chan"), P(None, "chan", None), P("space", None, None), P(None, "space"))
    out_specs = P("space", "chan")
    return jax.shard_map(
        functools.partial(local, grid_rows), mesh=mesh, in_specs=in_specs, out_specs=out_specs, check_vma=False
    )
```

```python
import functools

import jax
import jax.numpy as jnp
from jax import lax
from jax.experimental import pallas as pl
from jax.experimental.pallas import tpu as pltpu
from jax.sharding import PartitionSpec as P

GRID_COLS = 8
MESH = pl.DeviceIdType.MESH
DIRECTIONS = [(-1, -1), (-1, 0), (-1, 1), (0, -1), (0, 1), (1, -1), (1, 0), (1, 1)]
VERTICAL = {1: (0, 2), 6: (5, 7)}
HORIZONTAL = (3, 4)
LANES = 128
PIECES = 4
CHUNK = 256
GROUP = 32


def exchange(
    grid_rows, feat, send_rows, gmap, table, idx,
    blocks, rows, lut, blk_send, blk_recv, row_send, row_recv,
):
    voxels = feat.shape[0]
    offsets = gmap.shape[0]
    slot_tiles = rows.shape[2] // LANES
    zero_row = 9 * voxels
    piece = voxels // PIECES
    me = lax.axis_index("space")
    chan = lax.axis_index("chan")
    my_row = me // GRID_COLS
    my_col = me % GRID_COLS

    def inside(dx, dy):
        row, col = my_row + dx, my_col + dy
        return (row >= 0) & (row < grid_rows) & (col >= 0) & (col < GRID_COLS)

    def device(dx, dy):
        return (me + dx * GRID_COLS + dy, chan)

    def block_copy(src, slot, part, dx, dy):
        return pltpu.make_async_remote_copy(
            src_ref=src.at[pl.ds(part * piece, piece)],
            dst_ref=blocks.at[slot, pl.ds(part * piece, piece)],
            send_sem=blk_send.at[slot, part],
            recv_sem=blk_recv.at[slot, part],
            device_id=device(dx, dy),
            device_id_type=MESH,
        )

    def rows_copy(slot, dx, dy):
        return pltpu.make_async_remote_copy(
            src_ref=send_rows.at[0, pl.ds(slot, 1)],
            dst_ref=rows.at[slot],
            send_sem=row_send.at[slot],
            recv_sem=row_recv.at[slot],
            device_id=device(dx, dy),
            device_id_type=MESH,
        )

    rows[...] = jnp.full(rows.shape, voxels, jnp.int32)

    barrier = pltpu.get_barrier_semaphore()
    expected = jnp.int32(0)
    for dx, dy in DIRECTIONS:
        expected = expected + inside(dx, dy).astype(jnp.int32)

        @pl.when(inside(dx, dy))
        def _():
            pl.semaphore_signal(barrier, inc=1, device_id=device(dx, dy), device_id_type=MESH)

    pl.semaphore_wait(barrier, expected)

    for part in range(PIECES):
        for slot in VERTICAL:
            dx, dy = DIRECTIONS[slot]

            @pl.when(inside(dx, dy))
            def _():
                if part == 0:
                    rows_copy(slot, dx, dy).start()
                block_copy(feat, slot, part, dx, dy).start()

    for slot, (dx, dy) in enumerate(DIRECTIONS):
        if slot in VERTICAL:
            continue

        @pl.when(inside(dx, dy))
        def _():
            rows_copy(slot, dx, dy).start()
            if slot in HORIZONTAL:
                for part in range(PIECES):
                    block_copy(feat, slot, part, dx, dy).start()

    def widen(src, number, part):
        table[pl.ds(number * voxels + part * piece, piece), :] = src[pl.ds(part * piece, piece), :].astype(jnp.float32)

    table[pl.ds(zero_row, 8), :] = jnp.zeros((8, LANES), jnp.float32)
    for part in range(PIECES):
        widen(feat, 0, part)

    for slot, (dx, dy) in enumerate(DIRECTIONS):
        @pl.when(inside(-dx, -dy))
        def _():
            rows_copy(slot, -dx, -dy).wait_recv()

        entry = rows[slot]
        lut[slot] = jnp.where(entry < voxels, entry + (1 + slot) * voxels, zero_row)

    own_tiles = voxels // LANES
    chunk_tiles = CHUNK // LANES
    for chunk in range(voxels // CHUNK):
        idx[chunk, pl.ds(idx.shape[1] - 8, 8), :] = jnp.full((8, CHUNK), zero_row, jnp.int32)

    def compose(col, _):
        lanes = pl.ds(pl.multiple_of(col * LANES, LANES), LANES)
        starts = list(range(0, offsets - 7, 8))
        if offsets % 8:
            starts.append(offsets - 8)
        entries = [gmap[pl.ds(start, 8), lanes] for start in starts]
        within = [entry & (LANES - 1) for entry in entries]
        tiles = [entry >> 7 for entry in entries]
        result = [jnp.where(entry < voxels, entry, zero_row) for entry in entries]
        for slot in range(8):
            for tile in range(slot_tiles):
                line = jnp.broadcast_to(lut[slot, :, pl.ds(tile * LANES, LANES)], (8, LANES))
                number = own_tiles + slot * slot_tiles + tile
                for i in range(len(starts)):
                    found = jnp.take_along_axis(line, within[i], axis=1, mode="promise_in_bounds")
                    result[i] = jnp.where(tiles[i] == number, found, result[i])
        for start, value in zip(starts, result):
            idx[col // chunk_tiles, pl.ds(start, 8), pl.ds(pl.multiple_of(col % chunk_tiles * LANES, LANES), LANES)] = value
        return 0

    lax.fori_loop(0, own_tiles, compose, 0)

    for part in range(PIECES):
        for slot, (left, right) in VERTICAL.items():
            dx, dy = DIRECTIONS[slot]

            @pl.when(inside(-dx, -dy))
            def _():
                block_copy(feat, slot, part, -dx, -dy).wait_recv()
                for target, step in ((left, -1), (right, 1)):
                    @pl.when(inside(0, step))
                    def _():
                        block_copy(blocks.at[slot], target, part, 0, step).start()

                widen(blocks.at[slot], 1 + slot, part)

    for slot in HORIZONTAL + (0, 2, 5, 7):
        dx, dy = DIRECTIONS[slot]

        @pl.when(inside(-dx, -dy))
        def _():
            for part in range(PIECES):
                block_copy(feat, slot, part, -dx, -dy).wait_recv()
                widen(blocks.at[slot], 1 + slot, part)

    for slot, (dx, dy) in enumerate(DIRECTIONS):
        @pl.when(inside(dx, dy))
        def _():
            rows_copy(slot, dx, dy).wait_send()
            if slot in VERTICAL or slot in HORIZONTAL:
                for part in range(PIECES):
                    block_copy(feat, slot, part, dx, dy).wait_send()

    for slot, targets in VERTICAL.items():
        dx, dy = DIRECTIONS[slot]
        for target, step_y in zip(targets, (-1, 1)):
            @pl.when(inside(-dx, -dy) & inside(0, step_y))
            def _():
                for part in range(PIECES):
                    block_copy(feat, target, part, 0, step_y).wait_send()


def convolve(paired, table, idx, feat, weights, out, idx_s, buf_a, buf_b, acc, own, outgoing, incoming, idx_sem, part_send, part_recv):
    voxels = feat.shape[0]
    offsets = weights.shape[0]
    me = lax.axis_index("space")
    chan = lax.axis_index("chan")
    to_scalar = pltpu.make_async_copy(idx, idx_s, idx_sem)
    to_scalar.start()
    if paired:
        barrier = pltpu.get_barrier_semaphore()
        pl.semaphore_signal(barrier, inc=1, device_id=(me, 1 - chan), device_id_type=MESH)
        pl.semaphore_wait(barrier, 1)
    to_scalar.wait()

    centre = offsets // 2
    pairs = centre

    def offset_of(number):
        return number + (number >= centre).astype(jnp.int32)

    def gather(buf, pair, chunk):
        for half in range(2):
            offset = offset_of(2 * pair + half)
            for first in range(0, CHUNK, GROUP):
                taken = [table[idx_s[chunk, offset, first + v]] for v in range(GROUP)]
                for v in range(GROUP):
                    buf[pl.ds(first + v, 1), pl.ds(half * LANES, LANES)] = taken[v]

    def product(buf, pair):
        kernel_pair = jnp.concatenate([weights[offset_of(2 * pair)], weights[offset_of(2 * pair + 1)]], axis=0)
        acc[...] += jnp.dot(buf[...].astype(jnp.bfloat16), kernel_pair, preferred_element_type=jnp.float32)

    other = pl.ds(pl.multiple_of((1 - chan) * LANES, LANES), LANES)
    mine = pl.ds(pl.multiple_of(chan * LANES, LANES), LANES)

    def partial_copy(chunk):
        span = pl.ds(pl.multiple_of(chunk * CHUNK, CHUNK), CHUNK)
        return pltpu.make_async_remote_copy(
            src_ref=outgoing.at[span],
            dst_ref=incoming.at[span],
            send_sem=part_send.at[chunk],
            recv_sem=part_recv.at[chunk],
            device_id=(me, 1 - chan),
            device_id_type=MESH,
        )

    def step(chunk, _):
        span = pl.ds(pl.multiple_of(chunk * CHUNK, CHUNK), CHUNK)
        acc[...] = jnp.dot(feat[span, :], weights[centre], preferred_element_type=jnp.float32)
        gather(buf_a, jnp.int32(0), chunk)

        def two(i, _):
            product(buf_a, 2 * i)
            gather(buf_b, 2 * i + 1, chunk)
            product(buf_b, 2 * i + 1)
            gather(buf_a, 2 * i + 2, chunk)
            return 0

        lax.fori_loop(0, (pairs - 1) // 2, two, 0)
        product(buf_a, jnp.int32(pairs - 1))
        if not paired:
            out[span, :] = acc[...]
            return 0
        own[span, :] = acc[:, mine]
        outgoing[span, :] = acc[:, other]
        partial_copy(chunk).start()
        return 0

    chunks = voxels // CHUNK
    lax.fori_loop(0, chunks, step, 0)

    def finish(chunk, _):
        span = pl.ds(pl.multiple_of(chunk * CHUNK, CHUNK), CHUNK)
        partial_copy(chunk).wait()
        out[span, :] = (own[span, :] + incoming[span, :]).astype(out.dtype)
        return 0

    if paired:
        lax.fori_loop(0, chunks, finish, 0)


def local(grid_rows, features, weights, send_rows, gather_map):
    voxels, own_width = features.shape
    offsets = gather_map.shape[0]
    out_width = weights.shape[2]
    slots = send_rows.shape[2]
    paired = lax.axis_size("chan") == 2 and own_width == LANES
    if not paired:
        features = jnp.pad(features, ((0, 0), (0, LANES - own_width)))
        weights = jnp.pad(weights, ((0, 0), (0, LANES - own_width), (0, 0)))
    width = LANES
    chunks = voxels // CHUNK
    maps = (chunks, pl.cdiv(offsets, 8) * 8, CHUNK)
    dma = pltpu.SemaphoreType.DMA
    result = jax.ShapeDtypeStruct((voxels, width) if paired else (voxels, out_width), jnp.bfloat16 if paired else jnp.float32)
    vmem = pl.BlockSpec(memory_space=pltpu.VMEM)
    table, idx = pl.pallas_call(
        functools.partial(exchange, grid_rows),
        out_shape=(
            jax.ShapeDtypeStruct((9 * voxels + 8, width), jnp.float32),
            jax.ShapeDtypeStruct(maps, jnp.int32),
        ),
        in_specs=[vmem] * 3,
        out_specs=(vmem, vmem),
        scratch_shapes=[
            pltpu.VMEM((8, voxels, width), jnp.bfloat16),
            pltpu.VMEM((8, 1, slots), jnp.int32),
            pltpu.VMEM((8, 1, slots), jnp.int32),
            dma((8, PIECES)), dma((8, PIECES)), dma((8,)), dma((8,)),
        ],
        compiler_params=pltpu.CompilerParams(
            collective_id=0, has_side_effects=True, vmem_limit_bytes=20 * 1024 * 1024
        ),
        cost_estimate=pl.CostEstimate(flops=0, bytes_accessed=64 * 1024 * 1024, transcendentals=0),
    )(features, send_rows, gather_map)
    made = pl.pallas_call(
        functools.partial(convolve, paired),
        out_shape=result,
        in_specs=[vmem] * 4,
        out_specs=vmem,
        scratch_shapes=[
            pltpu.SMEM(maps, jnp.int32),
            pltpu.VMEM((CHUNK, 2 * width), jnp.float32),
            pltpu.VMEM((CHUNK, 2 * width), jnp.float32),
            pltpu.VMEM((CHUNK, out_width), jnp.float32),
            pltpu.VMEM((voxels, width), jnp.float32),
            pltpu.VMEM((voxels, width), jnp.float32),
            pltpu.VMEM((voxels, width), jnp.float32),
            dma, dma((chunks,)), dma((chunks,)),
        ],
        compiler_params=pltpu.CompilerParams(
            collective_id=1 if paired else None, has_side_effects=paired, vmem_limit_bytes=24 * 1024 * 1024
        ),
        cost_estimate=pl.CostEstimate(
            flops=2 * voxels * offsets * width * out_width, bytes_accessed=8 * 1024 * 1024, transcendentals=0
        ),
    )(table.reshape(9 * voxels + 8, 1, width), idx, features, weights)
    if paired:
        return made
    return lax.psum_scatter(made, "chan", scatter_dimension=1, tiled=True).astype(jnp.bfloat16)


def solution(mesh):
    grid_rows = mesh.shape["space"] // GRID_COLS
    in_specs = (P("space", "chan"), P(None, "chan", None), P("space", None, None), P(None, "space"))
    out_specs = P("space", "chan")
    return jax.shard_map(
        functools.partial(local, grid_rows), mesh=mesh, in_specs=in_specs, out_specs=out_specs, check_vma=False
    )
```

```python
import functools

import jax
import jax.numpy as jnp
from jax import lax
from jax.experimental import pallas as pl
from jax.experimental.pallas import tpu as pltpu
from jax.sharding import PartitionSpec as P

GRID_COLS = 8
MESH = pl.DeviceIdType.MESH
DIRECTIONS = [(-1, -1), (-1, 0), (-1, 1), (0, -1), (0, 1), (1, -1), (1, 0), (1, 1)]
VERTICAL = {1: (0, 2), 6: (5, 7)}
HORIZONTAL = (3, 4)
LANES = 128
PIECES = 4
CHUNK = 256
GROUP = 32


def kernel(
    grid_rows, paired, feat_hbm, weights_hbm, send_rows, gmap_hbm, out,
    feat, weights, gmap, blocks, rows, lut, table, idx, idx_s, buf_a, buf_b, acc, own, outgoing, incoming,
    blk_send, blk_recv, row_send, row_recv, in_sem, idx_sem, part_send, part_recv,
):
    voxels = feat.shape[0]
    offsets = gmap.shape[0]
    slot_tiles = rows.shape[2] // LANES
    zero_row = 9 * voxels
    piece = voxels // PIECES
    me = lax.axis_index("space")
    chan = lax.axis_index("chan")
    my_row = me // GRID_COLS
    my_col = me % GRID_COLS

    def inside(dx, dy):
        row, col = my_row + dx, my_col + dy
        return (row >= 0) & (row < grid_rows) & (col >= 0) & (col < GRID_COLS)

    def device(dx, dy):
        return (me + dx * GRID_COLS + dy, chan)

    def block_copy(src, slot, part, dx, dy):
        return pltpu.make_async_remote_copy(
            src_ref=src.at[pl.ds(part * piece, piece)],
            dst_ref=blocks.at[slot, pl.ds(part * piece, piece)],
            send_sem=blk_send.at[slot, part],
            recv_sem=blk_recv.at[slot, part],
            device_id=device(dx, dy),
            device_id_type=MESH,
        )

    def rows_copy(slot, dx, dy):
        return pltpu.make_async_remote_copy(
            src_ref=send_rows.at[0, pl.ds(slot, 1)],
            dst_ref=rows.at[slot],
            send_sem=row_send.at[slot],
            recv_sem=row_recv.at[slot],
            device_id=device(dx, dy),
            device_id_type=MESH,
        )

    staged = [
        pltpu.make_async_copy(source, target, in_sem.at[number])
        for number, (source, target) in enumerate(((feat_hbm, feat), (gmap_hbm, gmap), (weights_hbm, weights)))
    ]
    for copy in staged:
        copy.start()

    rows[...] = jnp.full(rows.shape, voxels, jnp.int32)

    barrier = pltpu.get_barrier_semaphore()
    expected = jnp.int32(1 if paired else 0)
    for dx, dy in DIRECTIONS:
        expected = expected + inside(dx, dy).astype(jnp.int32)

        @pl.when(inside(dx, dy))
        def _():
            pl.semaphore_signal(barrier, inc=1, device_id=device(dx, dy), device_id_type=MESH)

    if paired:
        pl.semaphore_signal(barrier, inc=1, device_id=(me, 1 - chan), device_id_type=MESH)
    pl.semaphore_wait(barrier, expected)

    for part in range(PIECES):
        for slot in VERTICAL:
            dx, dy = DIRECTIONS[slot]

            @pl.when(inside(dx, dy))
            def _():
                if part == 0:
                    rows_copy(slot, dx, dy).start()
                block_copy(feat_hbm, slot, part, dx, dy).start()

    for slot, (dx, dy) in enumerate(DIRECTIONS):
        if slot in VERTICAL:
            continue

        @pl.when(inside(dx, dy))
        def _():
            rows_copy(slot, dx, dy).start()
            if slot in HORIZONTAL:
                for part in range(PIECES):
                    block_copy(feat_hbm, slot, part, dx, dy).start()

    def widen(src, number, part):
        table[pl.ds(number * voxels + part * piece, piece), :] = src[pl.ds(part * piece, piece), :].astype(jnp.float32)

    table[pl.ds(zero_row, 8), :] = jnp.zeros((8, LANES), jnp.float32)
    staged[0].wait()
    for part in range(PIECES):
        widen(feat, 0, part)
    staged[1].wait()

    for slot, (dx, dy) in enumerate(DIRECTIONS):
        @pl.when(inside(-dx, -dy))
        def _():
            rows_copy(slot, -dx, -dy).wait_recv()

        entry = rows[slot]
        lut[slot] = jnp.where(entry < voxels, entry + (1 + slot) * voxels, zero_row)

    own_tiles = voxels // LANES
    chunk_tiles = CHUNK // LANES
    for chunk in range(voxels // CHUNK):
        idx[chunk, pl.ds(idx.shape[1] - 8, 8), :] = jnp.full((8, CHUNK), zero_row, jnp.int32)

    def compose(col, _):
        lanes = pl.ds(pl.multiple_of(col * LANES, LANES), LANES)
        starts = list(range(0, offsets - 7, 8))
        if offsets % 8:
            starts.append(offsets - 8)
        entries = [gmap[pl.ds(start, 8), lanes] for start in starts]
        within = [entry & (LANES - 1) for entry in entries]
        tiles = [entry >> 7 for entry in entries]
        result = [jnp.where(entry < voxels, entry, zero_row) for entry in entries]
        for slot in range(8):
            for tile in range(slot_tiles):
                line = jnp.broadcast_to(lut[slot, :, pl.ds(tile * LANES, LANES)], (8, LANES))
                number = own_tiles + slot * slot_tiles + tile
                for i in range(len(starts)):
                    found = jnp.take_along_axis(line, within[i], axis=1, mode="promise_in_bounds")
                    result[i] = jnp.where(tiles[i] == number, found, result[i])
        for start, value in zip(starts, result):
            idx[col // chunk_tiles, pl.ds(start, 8), pl.ds(pl.multiple_of(col % chunk_tiles * LANES, LANES), LANES)] = value
        return 0

    lax.fori_loop(0, own_tiles, compose, 0)
    to_scalar = pltpu.make_async_copy(idx, idx_s, idx_sem)
    to_scalar.start()

    for part in range(PIECES):
        for slot, (left, right) in VERTICAL.items():
            dx, dy = DIRECTIONS[slot]

            @pl.when(inside(-dx, -dy))
            def _():
                block_copy(feat, slot, part, -dx, -dy).wait_recv()
                for target, step in ((left, -1), (right, 1)):
                    @pl.when(inside(0, step))
                    def _():
                        block_copy(blocks.at[slot], target, part, 0, step).start()

                widen(blocks.at[slot], 1 + slot, part)

    for slot in HORIZONTAL + (0, 2, 5, 7):
        dx, dy = DIRECTIONS[slot]

        @pl.when(inside(-dx, -dy))
        def _():
            for part in range(PIECES):
                block_copy(feat, slot, part, -dx, -dy).wait_recv()
                widen(blocks.at[slot], 1 + slot, part)

    to_scalar.wait()
    staged[2].wait()

    centre = offsets // 2
    pairs = centre

    def offset_of(number):
        return number + (number >= centre).astype(jnp.int32)

    def gather(buf, pair, chunk):
        for half in range(2):
            offset = offset_of(2 * pair + half)
            for first in range(0, CHUNK, GROUP):
                taken = [table[pl.ds(idx_s[chunk, offset, first + v], 1), :] for v in range(GROUP)]
                for v in range(GROUP):
                    buf[pl.ds(first + v, 1), pl.ds(half * LANES, LANES)] = taken[v]

    def product(buf, pair):
        kernel_pair = jnp.concatenate([weights[offset_of(2 * pair)], weights[offset_of(2 * pair + 1)]], axis=0)
        acc[...] += jnp.dot(buf[...].astype(jnp.bfloat16), kernel_pair, preferred_element_type=jnp.float32)

    other = pl.ds(pl.multiple_of((1 - chan) * LANES, LANES), LANES)
    mine = pl.ds(pl.multiple_of(chan * LANES, LANES), LANES)

    def partial_copy(chunk):
        span = pl.ds(pl.multiple_of(chunk * CHUNK, CHUNK), CHUNK)
        return pltpu.make_async_remote_copy(
            src_ref=outgoing.at[span],
            dst_ref=incoming.at[span],
            send_sem=part_send.at[chunk],
            recv_sem=part_recv.at[chunk],
            device_id=(me, 1 - chan),
            device_id_type=MESH,
        )

    def step(chunk, _):
        base = chunk * CHUNK
        span = pl.ds(pl.multiple_of(base, CHUNK), CHUNK)
        acc[...] = jnp.dot(feat[span, :], weights[centre], preferred_element_type=jnp.float32)
        gather(buf_a, jnp.int32(0), chunk)

        def two(i, _):
            product(buf_a, 2 * i)
            gather(buf_b, 2 * i + 1, chunk)
            product(buf_b, 2 * i + 1)
            gather(buf_a, 2 * i + 2, chunk)
            return 0

        lax.fori_loop(0, (pairs - 1) // 2, two, 0)
        product(buf_a, jnp.int32(pairs - 1))
        if not paired:
            out[span, :] = acc[...]
            return 0
        own[span, :] = acc[:, mine]
        outgoing[span, :] = acc[:, other]
        partial_copy(chunk).start()
        return 0

    chunks = voxels // CHUNK
    lax.fori_loop(0, chunks, step, 0)

    def finish(chunk, _):
        span = pl.ds(pl.multiple_of(chunk * CHUNK, CHUNK), CHUNK)
        partial_copy(chunk).wait()
        out[span, :] = (own[span, :] + incoming[span, :]).astype(out.dtype)
        return 0

    if paired:
        lax.fori_loop(0, chunks, finish, 0)

    for slot, (dx, dy) in enumerate(DIRECTIONS):
        @pl.when(inside(dx, dy))
        def _():
            rows_copy(slot, dx, dy).wait_send()
            if slot in VERTICAL or slot in HORIZONTAL:
                for part in range(PIECES):
                    block_copy(feat, slot, part, dx, dy).wait_send()

    for slot, targets in VERTICAL.items():
        dx, dy = DIRECTIONS[slot]
        for target, step_y in zip(targets, (-1, 1)):
            @pl.when(inside(-dx, -dy) & inside(0, step_y))
            def _():
                for part in range(PIECES):
                    block_copy(feat, target, part, 0, step_y).wait_send()


def local(grid_rows, features, weights, send_rows, gather_map):
    voxels, own_width = features.shape
    offsets = gather_map.shape[0]
    out_width = weights.shape[2]
    slots = send_rows.shape[2]
    paired = lax.axis_size("chan") == 2 and own_width == LANES
    if not paired:
        features = jnp.pad(features, ((0, 0), (0, LANES - own_width)))
        weights = jnp.pad(weights, ((0, 0), (0, LANES - own_width), (0, 0)))
    width = LANES
    chunks = voxels // CHUNK
    maps = (chunks, pl.cdiv(offsets, 8) * 8, CHUNK)
    dma = pltpu.SemaphoreType.DMA
    result = jax.ShapeDtypeStruct((voxels, width) if paired else (voxels, out_width), jnp.bfloat16 if paired else jnp.float32)
    made = pl.pallas_call(
        functools.partial(kernel, grid_rows, paired),
        out_shape=result,
        in_specs=[pl.BlockSpec(memory_space=pl.ANY)] * 4,
        out_specs=pl.BlockSpec(memory_space=pltpu.VMEM),
        scratch_shapes=[
            pltpu.VMEM(features.shape, features.dtype),
            pltpu.VMEM(weights.shape, weights.dtype),
            pltpu.VMEM(gather_map.shape, gather_map.dtype),
            pltpu.VMEM((8, voxels, width), jnp.bfloat16),
            pltpu.VMEM((8, 1, slots), jnp.int32),
            pltpu.VMEM((8, 1, slots), jnp.int32),
            pltpu.VMEM((9 * voxels + 8, width), jnp.float32),
            pltpu.VMEM(maps, jnp.int32),
            pltpu.SMEM(maps, jnp.int32),
            pltpu.VMEM((CHUNK, 2 * width), jnp.float32),
            pltpu.VMEM((CHUNK, 2 * width), jnp.float32),
            pltpu.VMEM((CHUNK, out_width), jnp.float32),
            pltpu.VMEM((voxels, width), jnp.float32),
            pltpu.VMEM((voxels, width), jnp.float32),
            pltpu.VMEM((voxels, width), jnp.float32),
            dma((8, PIECES)), dma((8, PIECES)), dma((8,)), dma((8,)), dma((3,)), dma, dma((chunks,)), dma((chunks,)),
        ],
        compiler_params=pltpu.CompilerParams(
            collective_id=0, has_side_effects=True, vmem_limit_bytes=64 * 1024 * 1024
        ),
        cost_estimate=pl.CostEstimate(
            flops=2 * voxels * offsets * width * out_width, bytes_accessed=6 * 1024 * 1024, transcendentals=0
        ),
    )(features, weights, send_rows, gather_map)
    if paired:
        return made
    return lax.psum_scatter(made, "chan", scatter_dimension=1, tiled=True).astype(jnp.bfloat16)


def solution(mesh):
    grid_rows = mesh.shape["space"] // GRID_COLS
    in_specs = (P("space", "chan"), P(None, "chan", None), P("space", None, None), P(None, "space"))
    out_specs = P("space", "chan")
    return jax.shard_map(
        functools.partial(local, grid_rows), mesh=mesh, in_specs=in_specs, out_specs=out_specs, check_vma=False
    )
```
